256 devices in a mesh: shot: 32 (over z, y_hi, core), surf: 8 (over x, y_lo).
Axes of the slice: x: 4, y: 4 (y_hi: 2, y_lo: 2; y = y_hi * 2 + y_lo), z: 8, core: 2. Of those that a mesh axis runs over, the one named last changes fastest.
Arguments:
- data: float32 [64, 512, 512], P('shot', 'surf'), may hold values from -6 to 6
- positions: int32 [512], P('surf'), may hold values from 0 to 255, as said below
- plan: int32 [32], replicated, may hold values from 0 to 31, each once
- primaries: bfloat16 [256, 16, 32, 256], P('surf', None, 'shot'), may hold values from -0.015625 to 0.015625
- scale: float32 [64], P('shot'), may hold values from 0.5 to 1.5
Outputs:
- demultiplied: float32 [64, 512, 512], P('shot', 'surf')
The draws below stay inside these ranges and needn't reach their ends.
Inputs may be any that keep to these rules, and one draw needn't show every extreme that they name: `positions`: receiver r lies at a position of the block [b * 32, (b + 1) * 32) with b = r // 64; in each such block of receivers the first maps to the block's first position and the last to its last. A permutation: slot i of primaries holds receiver panel plan[i].
All inputs are finite; a program needn't handle non-finite values.
Results may differ from the reference program's by a relative error of at most 0.0065.
Values may be sent and summed in bfloat16 or wider, within the bound.
No kernel may reach another device: no remote copies, remote signals or barrier semaphores. Data moves between devices by JAX's collectives and lax.ppermute only.
A program may use at most 128 MiB of HBM per device.

```python
import math
import jax
import jax.numpy as jnp
from jax import lax

S_DEV = 2
PD = 32
RP = 16
NT = 512
TAPS = 256
PANELS = 32
SHOTS = 64
RECV = 512
RECV_DEV = 64
POSITIONS = 256
N_SURF = 8


def draw_positions(key, part):
    receiver_index = jnp.arange(RECV, dtype=jnp.int32)
    offset = receiver_index % RECV_DEV
    block_index = receiver_index // RECV_DEV
    picked = jax.random.randint(key, (RECV,), 0, PD, dtype=jnp.int32)
    picked = jnp.where(offset == 0, 0, jnp.where(offset == RECV_DEV - 1, PD - 1, picked))
    return (block_index * PD + picked).astype(jnp.int32)


def levels(rng, shape, cuts, smallest, top_value):
    def one(axis_at, blocks):
        heights = jax.random.uniform(jax.random.fold_in(jax.random.fold_in(rng, 6), axis_at), (blocks,), jnp.float32, smallest / len(cuts), top_value / len(cuts))
        return jnp.repeat(jnp.exp(heights), shape[axis_at] // blocks).reshape((-1,) + (1,) * (len(shape) - axis_at - 1))

    gain = one(*cuts[0])
    for cut in cuts[1:]:
        gain = gain * one(*cut)
    return gain


def centred(rng, dims, width, limit, pieces=(), held_as=jnp.bfloat16):
    loudness = levels(rng, dims, pieces, -0.22, 0.18) if pieces else 1.0
    drawn = jax.random.normal(rng, dims, jnp.float32) * width * loudness
    return jnp.minimum(jnp.maximum(drawn, -limit), limit).astype(held_as)


def setup_inputs(seed: int = 0) -> dict:
    arg_keys = jax.random.split(jax.random.key(seed), 6)
    return {
        "data": centred(arg_keys[0], (SHOTS, RECV, NT), 1.0, 6.0, ((0, 32), (1, 8)), jnp.float32),
        "positions": draw_positions(jax.random.fold_in(arg_keys[5], 71), 0),
        "plan": jax.random.permutation(arg_keys[2], PANELS).astype(jnp.int32),
        "primaries": centred(arg_keys[3], (POSITIONS, RP, PANELS, TAPS), (2 * POSITIONS * TAPS) ** -0.5, 0.015625, ((0, 8), (2, 32))),
        "scale": jnp.clip(jnp.exp(math.log(1.5) - 1.0986123 * jax.random.uniform(arg_keys[4], (SHOTS,), jnp.float32) ** levels(arg_keys[4], (SHOTS,), ((0, 32),), -0.2, 0.2)), 0.5, 1.5),
    }


def fourier_matrices(samples):
    length = 2 * samples
    time_index = jnp.arange(samples, dtype=jnp.int32)
    phase_index = (time_index[:, None] * time_index[None, :]) % length
    angles = phase_index.astype(jnp.float32) * (2.0 * math.pi / length)
    cosine = jnp.cos(angles)
    sine_part = jnp.sin(angles)
    alternate = (1 - 2 * (time_index % 2)).astype(jnp.float32)
    nyquist = time_index == 0
    forward_imag = jnp.where(nyquist[None, :], alternate[:, None], -sine_part)
    forward = jnp.concatenate([cosine, forward_imag], axis=1).astype(jnp.bfloat16)
    weights = jnp.where(nyquist, 1.0, 2.0).astype(jnp.float32) / length
    backward_real_table = cosine.T * weights[:, None]
    inverse_imag = jnp.where(nyquist[:, None], alternate[None, :] / length, -2.0 * sine_part.T / length)
    inverse = jnp.concatenate([backward_real_table, inverse_imag], axis=0).astype(jnp.bfloat16)
    return forward, inverse


def spectral_product(left, right):
    half = left.shape[-1] // 2
    left_real = left[..., :half]
    left_imag = left[..., half:]
    right_real = right[..., :half]
    right_imag = right[..., half:]

    def contract(leading_factor, trailing_factor):
        return jnp.einsum("quw,ugw->qgw", leading_factor, trailing_factor, precision=lax.Precision.HIGHEST)

    real_cross_term = contract(left_real, right_real)
    imaginary_cross_term = contract(left_imag, right_imag)
    crossed = contract(left_real, right_imag) + contract(left_imag, right_real)
    interior = (jnp.arange(half) > 0).astype(jnp.float32)
    return jnp.concatenate([real_cross_term - interior * imaginary_cross_term, interior * crossed + (1.0 - interior) * imaginary_cross_term], axis=-1)


def reference(data, positions, plan, primaries, scale):
    shot_total, receiver_total, samples = data.shape
    position_total = primaries.shape[0]
    tap_count = primaries.shape[3]
    forward, inverse = fourier_matrices(samples)
    onehot = (positions[:, None] == jnp.arange(position_total, dtype=jnp.int32)[None, :]).astype(jnp.float32)
    gathered = jnp.einsum("srt,rx->sxt", data, onehot, precision=lax.Precision.HIGHEST).astype(jnp.bfloat16)
    data_spectra = jnp.dot(gathered.reshape(-1, samples), forward, preferred_element_type=jnp.float32)
    data_spectra = data_spectra.astype(jnp.bfloat16).reshape(shot_total, position_total, 2 * samples)
    panel_order = jnp.argsort(plan).astype(jnp.int32)
    arranged = jnp.take(primaries, panel_order, axis=2)
    primary_spectra = jnp.dot(arranged.reshape(-1, tap_count), forward[:tap_count], preferred_element_type=jnp.float32)
    primary_spectra = primary_spectra.astype(jnp.bfloat16).astype(jnp.float32).reshape(position_total, receiver_total, 2 * samples)

    def one_group(group_spectra):
        group_wide = group_spectra.astype(jnp.float32)
        running = jnp.zeros((group_spectra.shape[0], receiver_total, 2 * samples), jnp.float32)
        for block_index in range(N_SURF):
            low = block_index * PD
            term = spectral_product(group_wide[:, low:low + PD], primary_spectra[low:low + PD])
            rounded = lax.optimization_barrier(term.astype(jnp.bfloat16))
            running = running + rounded.astype(jnp.float32)
        spectrum = running.astype(jnp.bfloat16)
        in_time = jnp.dot(spectrum.reshape(-1, 2 * samples), inverse, preferred_element_type=jnp.float32)
        return in_time.reshape(group_spectra.shape[0], receiver_total, samples)

    grouped = data_spectra.reshape(shot_total // S_DEV, S_DEV, position_total, 2 * samples)
    prediction = lax.map(one_group, grouped).reshape(shot_total, receiver_total, samples)
    return data - scale[:, None, None] * prediction
```

```python
import math

import jax
import jax.numpy as jnp
import ml_dtypes
import numpy as np
from jax import lax
from jax.experimental import pallas as pl
from jax.experimental.pallas import tpu as pltpu

LANES = 128
NT_DIMS = (((1,), (1,)), ((), ()))


def fourier_tables(taps):
    length = 2 * taps
    frequency = np.arange(taps)[:, None]
    time = np.arange(length)[None, :]
    angle = (frequency * time % length) * (2.0 * math.pi / length)
    cosine, sine = np.cos(angle), np.sin(angle)
    alternate = 1.0 - 2.0 * (time % 2)
    packed = frequency == 0
    forward = np.concatenate([cosine, np.where(packed, alternate, -sine)], axis=0)
    weight = np.where(packed, 1.0, 2.0) / length
    inverse_real = (weight * cosine)[:, taps:]
    inverse_imag = np.where(packed, alternate / length, -2.0 * sine / length)[:, taps:]
    inverse = np.concatenate([inverse_real, inverse_imag], axis=1)
    return forward.astype(ml_dtypes.bfloat16), inverse.astype(ml_dtypes.bfloat16)


def exchange_groups(parts):
    lane = lax.broadcasted_iota(jnp.int32, parts[0].shape, 1)
    parts = list(parts)
    for bit in (1, 2):
        shift = bit * 32
        high = (lane & shift) != 0
        swapped = [None] * 4
        for low_index in range(4):
            if low_index & bit:
                continue
            low, top = parts[low_index], parts[low_index | bit]
            swapped[low_index] = jnp.where(high, pltpu.roll(top, shift, 1), low)
            swapped[low_index | bit] = jnp.where(high, top, pltpu.roll(low, LANES - shift, 1))
        parts = swapped
    return parts


def spectra_kernel(positions, data, primaries, forward, sent, rows, packed):
    shots, _, samples = data.shape
    position_count, width, taps = primaries.shape
    row_count = position_count * width
    frequencies = taps
    chunk = packed.shape[0] // frequencies
    groups = width // 4
    tap_table = forward[:, :taps]
    flat = primaries[...].reshape(row_count, taps)
    tiles = range(taps // LANES)
    for tile in tiles:
        rows[tile] = flat[:, tile * LANES : (tile + 1) * LANES].astype(jnp.float32)
    for group in range(groups):
        block = jnp.concatenate(
            [
                jnp.concatenate(
                    [rows[tile, pl.ds(4 * group + j, position_count, stride=width), :] for tile in tiles],
                    axis=1,
                )
                for j in range(4)
            ],
            axis=0,
        ).astype(jnp.bfloat16)
        spectra = lax.dot_general(tap_table, block, NT_DIMS, preferred_element_type=jnp.float32)
        for part in range(2):
            packed[pl.ds(part * groups + group, frequencies, stride=chunk), :] = spectra[
                part * frequencies : (part + 1) * frequencies
            ]
    place = lax.broadcasted_iota(jnp.int32, (position_count, positions.shape[1]), 0)
    onehot = (place == positions[...]).astype(jnp.float32)
    windows = []
    for shot in range(shots):
        gathered = jnp.dot(
            onehot, data[shot], precision=lax.Precision.HIGHEST, preferred_element_type=jnp.float32
        ).astype(jnp.bfloat16)
        before = jnp.zeros((position_count, taps), jnp.bfloat16)
        windows.append(jnp.concatenate([before, gathered[:, :taps]], axis=1))
        windows.append(gathered)
    window = jnp.concatenate(windows, axis=0)
    spectra = lax.dot_general(forward[...], window, NT_DIMS, preferred_element_type=jnp.float32)
    for part in range(2):
        packed[pl.ds(2 * groups + part, frequencies, stride=chunk), :] = spectra[
            part * frequencies : (part + 1) * frequencies
        ]
    sent[...] = packed[...].astype(jnp.bfloat16)


def product_kernel(shot_devices, surf_devices, width, received, sent, rows, packed):
    rows[...] = received[...].astype(jnp.float32)
    chunk = received.shape[0] // (shot_devices * surf_devices)
    groups = width // 4

    def regrouped(row):
        halves = []
        for half in range(surf_devices // 4):
            parts = [
                rows[pl.ds((half * 4 + i) * chunk + row, shot_devices, stride=surf_devices * chunk), :]
                for i in range(4)
            ]
            halves.append(exchange_groups(parts))
        return [
            jnp.concatenate([half[j] for half in halves], axis=1).astype(jnp.bfloat16) for j in range(4)
        ]

    primary = []
    for part in range(2):
        by_receiver = []
        for group in range(groups):
            by_receiver += regrouped(part * groups + group)
        primary.append(by_receiver)
    traces = [jnp.concatenate(regrouped(2 * groups + part), axis=0) for part in range(2)]
    frequency = lax.axis_index("shot") * surf_devices + lax.axis_index("surf")
    interior = frequency > 0
    pair = width // surf_devices
    for block in range(surf_devices):
        which = range(pair * block, pair * (block + 1))
        real = jnp.concatenate([primary[0][q] for q in which], axis=0)
        imag = jnp.concatenate([primary[1][q] for q in which], axis=0)
        none = jnp.zeros_like(imag)
        with_real = jnp.concatenate([real, jnp.where(interior, imag, none)], axis=0)
        with_imag = jnp.concatenate(
            [jnp.where(interior, -imag, none), jnp.where(interior, real, imag)], axis=0
        )
        product = lax.dot_general(
            traces[0], with_real, NT_DIMS, preferred_element_type=jnp.float32
        ) + lax.dot_general(traces[1], with_imag, NT_DIMS, preferred_element_type=jnp.float32)
        for window in range(4):
            packed[pl.ds(block * 4 + window, shot_devices, stride=surf_devices * 4), :] = product[
                window * shot_devices : (window + 1) * shot_devices
            ]
    sent[...] = packed[...].astype(jnp.bfloat16)


def subtract_kernel(place, scale, received, inverse, data, out, rows):
    shots, receivers, _ = data.shape
    frequencies, columns = inverse.shape
    taps = columns // 2
    windows = received.shape[0] // frequencies
    rows[...] = received[...].astype(jnp.float32)
    order = (lax.broadcasted_iota(jnp.int32, (LANES, LANES), 0) == place[...]).astype(jnp.bfloat16)
    for window in range(windows):
        spectra = rows[pl.ds(window, frequencies, stride=windows), :].astype(jnp.bfloat16)
        turned = lax.dot_general(order, spectra, NT_DIMS, preferred_element_type=jnp.float32).astype(
            jnp.bfloat16
        )
        in_time = jnp.dot(
            turned[:receivers], inverse[:, :taps], preferred_element_type=jnp.float32
        ) + jnp.dot(turned[receivers:], inverse[:, taps:], preferred_element_type=jnp.float32)
        shot, half = divmod(window, windows // shots)
        span = slice(half * taps, (half + 1) * taps)
        out[shot, :, span] = data[shot, :, span] - scale[shot] * in_time


def on_device(shot_devices, surf_devices, data, positions, plan, primaries, scale):
    shots, receivers, samples = data.shape
    position_count, width, _, taps = primaries.shape
    devices = shot_devices * surf_devices
    forward, inverse = fourier_tables(taps)
    forward, inverse = jnp.asarray(forward), jnp.asarray(inverse)
    local = (positions - lax.axis_index("surf") * position_count).reshape(1, receivers)
    chunk = (2 * width * position_count + 2 * 2 * shots * position_count) // LANES
    vmem = pl.BlockSpec(memory_space=pltpu.VMEM)
    smem = pl.BlockSpec(memory_space=pltpu.SMEM)
    limit = pltpu.CompilerParams(vmem_limit_bytes=32 * 1024 * 1024)

    sent = pl.pallas_call(
        spectra_kernel,
        out_shape=jax.ShapeDtypeStruct((taps * chunk, LANES), jnp.bfloat16),
        in_specs=[vmem] * 4,
        out_specs=vmem,
        scratch_shapes=[
            pltpu.VMEM((taps // LANES, position_count * width, LANES), jnp.float32),
            pltpu.VMEM((taps * chunk, LANES), jnp.float32),
        ],
        compiler_params=limit,
    )(local, data, primaries.reshape(position_count, width, taps), forward)
    sent = sent.reshape(devices, chunk // 2, 2, LANES)
    received = lax.all_to_all(sent, ("shot", "surf"), 0, 0, tiled=True)
    received = received.reshape(devices * chunk, LANES)

    back = devices * 4

    def product(*refs):
        product_kernel(shot_devices, surf_devices, width, *refs)

    terms = pl.pallas_call(
        product,
        out_shape=jax.ShapeDtypeStruct((back, LANES), jnp.bfloat16),
        in_specs=[vmem],
        out_specs=vmem,
        scratch_shapes=[
            pltpu.VMEM((devices * chunk, LANES), jnp.float32),
            pltpu.VMEM((back, LANES), jnp.float32),
        ],
        compiler_params=limit,
    )(received)
    terms = lax.all_to_all(terms.reshape(devices, 4, LANES), ("shot", "surf"), 0, 0, tiled=True)
    terms = terms.reshape(back, LANES)

    pair = width // surf_devices
    offset = jnp.arange(2 * pair, dtype=jnp.int32) * plan.shape[0]
    place = (offset[:, None] + plan[None, :]).reshape(1, LANES)
    return pl.pallas_call(
        subtract_kernel,
        out_shape=jax.ShapeDtypeStruct(data.shape, jnp.float32),
        in_specs=[vmem, smem, vmem, vmem, vmem],
        out_specs=vmem,
        scratch_shapes=[pltpu.VMEM((back, LANES), jnp.float32)],
        compiler_params=limit,
    )(place, scale, terms, inverse, data)


def solution(mesh):
    P = jax.sharding.PartitionSpec
    shot_devices, surf_devices = mesh.shape["shot"], mesh.shape["surf"]

    def device(*args):
        return on_device(shot_devices, surf_devices, *args)

    in_specs = (P("shot", "surf", None), P("surf"), P(), P("surf", None, "shot", None), P("shot"))
    out_specs = P("shot", "surf", None)
    return jax.shard_map(device, mesh=mesh, in_specs=in_specs, out_specs=out_specs, check_vma=False)
```

```python
import math

import jax
import jax.numpy as jnp
import ml_dtypes
import numpy as np
from jax import lax
from jax.experimental import pallas as pl
from jax.experimental.pallas import tpu as pltpu

LANES = 128
NT_DIMS = (((1,), (1,)), ((), ()))


def fourier_tables(taps):
    length = 2 * taps
    frequency = np.arange(taps)[:, None]
    time = np.arange(length)[None, :]
    angle = (frequency * time % length) * (2.0 * math.pi / length)
    cosine, sine = np.cos(angle), np.sin(angle)
    alternate = 1.0 - 2.0 * (time % 2)
    packed = frequency == 0
    forward = np.concatenate([cosine, np.where(packed, alternate, -sine)], axis=0)[:, :taps]
    weight = np.where(packed, 1.0, 2.0) / length
    inverse_real = (weight * cosine)[:, taps:]
    inverse_imag = np.where(packed, alternate / length, -2.0 * sine / length)[:, taps:]
    inverse = np.concatenate([inverse_real, inverse_imag], axis=0)
    return forward.astype(ml_dtypes.bfloat16), inverse.astype(ml_dtypes.bfloat16)


def exchange_groups(parts):
    lane = lax.broadcasted_iota(jnp.int32, parts[0].shape, 1)
    parts = list(parts)
    for bit in (1, 2):
        shift = bit * 32
        high = (lane & shift) != 0
        swapped = [None] * 4
        for low_index in range(4):
            if low_index & bit:
                continue
            low, top = parts[low_index], parts[low_index | bit]
            swapped[low_index] = jnp.where(high, pltpu.roll(top, shift, 1), low)
            swapped[low_index | bit] = jnp.where(high, top, pltpu.roll(low, LANES - shift, 1))
        parts = swapped
    return parts


def spectra_kernel(
    positions_in,
    plan_in,
    scale_in,
    data_in,
    primaries_in,
    forward_in,
    sent,
    place,
    gain,
    positions,
    plan,
    scale,
    data,
    primaries,
    forward,
    rows,
    packed,
    arrived,
):
    shots, _, samples = data.shape
    position_count, width, taps = primaries.shape
    row_count = position_count * width
    frequencies = taps
    chunk = packed.shape[0] // frequencies
    groups = width // 4

    def halves(far, near):
        half = far.shape[0] // 2
        return [(far.at[pl.ds(i * half, half)], near.at[pl.ds(i * half, half)]) for i in range(2)]

    pairs = halves(primaries_in, primaries) + halves(forward_in, forward) + halves(data_in, data)
    pairs += [(positions_in, positions), (plan_in, plan), (scale_in, scale)]
    copies = [pltpu.make_async_copy(far, near, arrived.at[i]) for i, (far, near) in enumerate(pairs)]
    for copy in copies:
        copy.start()

    for copy in copies[:2]:
        copy.wait()
    flat = primaries[...].reshape(row_count, taps)
    tiles = range(taps // LANES)
    for tile in tiles:
        rows[tile] = flat[:, tile * LANES : (tile + 1) * LANES].astype(jnp.float32)
    for copy in copies[2:4]:
        copy.wait()
    for group in range(groups):
        block = jnp.concatenate(
            [
                jnp.concatenate(
                    [rows[tile, pl.ds(4 * group + j, position_count, stride=width), :] for tile in tiles],
                    axis=1,
                )
                for j in range(4)
            ],
            axis=0,
        ).astype(jnp.bfloat16)
        spectra = lax.dot_general(forward[...], block, NT_DIMS, preferred_element_type=jnp.float32)
        for part in range(2):
            packed[pl.ds(part * groups + group, frequencies, stride=chunk), :] = spectra[
                part * frequencies : (part + 1) * frequencies
            ]

    for copy in copies[4:]:
        copy.wait()
    place[...] = jnp.concatenate([plan[...] + i * plan.shape[1] for i in range(4)], axis=1)
    for shot in range(shots):
        gain[pl.ds(shot, 1), :] = jnp.full((1, taps), scale[shot], jnp.float32)
    first = lax.axis_index("surf") * position_count
    position = lax.broadcasted_iota(jnp.int32, (position_count, positions.shape[1]), 0) + first
    onehot = (position == positions[...]).astype(jnp.float32)
    halves_in_time = []
    for shot in range(shots):
        gathered = jnp.dot(
            onehot, data[shot], precision=lax.Precision.HIGHEST, preferred_element_type=jnp.float32
        ).astype(jnp.bfloat16)
        halves_in_time += [gathered[:, :taps], gathered[:, taps:]]
    spectra = lax.dot_general(
        forward[...], jnp.concatenate(halves_in_time, axis=0), NT_DIMS, preferred_element_type=jnp.float32
    )
    odd = lax.broadcasted_iota(jnp.int32, spectra.shape, 0) % 2 == 1
    second = lax.broadcasted_iota(jnp.int32, spectra.shape, 1) % (2 * position_count) >= position_count
    earlier = jnp.where(second, pltpu.roll(spectra, position_count, 1), 0.0)
    spectra = earlier + jnp.where(odd, -spectra, spectra)
    for part in range(2):
        packed[pl.ds(2 * groups + part, frequencies, stride=chunk), :] = spectra[
            part * frequencies : (part + 1) * frequencies
        ]
    sent[...] = packed[...].astype(jnp.bfloat16)


def product_kernel(shot_devices, surf_devices, width, received, sent, rows, packed):
    rows[...] = received[...].astype(jnp.float32)
    chunk = received.shape[0] // (shot_devices * surf_devices)
    groups = width // 4

    def regrouped(row):
        halves = []
        for half in range(surf_devices // 4):
            parts = [
                rows[pl.ds((half * 4 + i) * chunk + row, shot_devices, stride=surf_devices * chunk), :].astype(
                    jnp.bfloat16
                )
                for i in range(4)
            ]
            halves.append(exchange_groups(parts))
        return [jnp.concatenate([half[j] for half in halves], axis=1) for j in range(4)]

    primary = []
    for part in range(2):
        by_receiver = []
        for group in range(groups):
            by_receiver += regrouped(part * groups + group)
        primary.append(by_receiver)
    traces = [jnp.concatenate(regrouped(2 * groups + part), axis=0) for part in range(2)]
    frequency = lax.axis_index("shot") * surf_devices + lax.axis_index("surf")
    interior = frequency > 0
    pair = width // surf_devices
    for block in range(surf_devices):
        which = range(pair * block, pair * (block + 1))
        real = jnp.concatenate([primary[0][q] for q in which], axis=0)
        imag = jnp.concatenate([primary[1][q] for q in which], axis=0)
        none = jnp.zeros_like(imag)
        with_real = jnp.concatenate([real, jnp.where(interior, imag, none)], axis=0)
        with_imag = jnp.concatenate(
            [jnp.where(interior, -imag, none), jnp.where(interior, real, imag)], axis=0
        )
        product = lax.dot_general(
            traces[0], with_real, NT_DIMS, preferred_element_type=jnp.float32
        ) + lax.dot_general(traces[1], with_imag, NT_DIMS, preferred_element_type=jnp.float32)
        for window in range(4):
            packed[pl.ds(block * 4 + window, shot_devices, stride=surf_devices * 4), :] = product[
                window * shot_devices : (window + 1) * shot_devices
            ]
    sent[...] = packed[...].astype(jnp.bfloat16)


def subtract_kernel(place, gain, received, inverse, data, out, rows, result, written):
    shots, receivers, _ = data.shape
    frequencies, taps = inverse.shape[0] // 2, inverse.shape[1]
    windows = received.shape[0] // frequencies
    rows[...] = received[...].astype(jnp.float32)
    order = (lax.broadcasted_iota(jnp.int32, (LANES, LANES), 0) == place[...]).astype(jnp.bfloat16)
    copies = []
    for shot in range(shots):
        spectra = jnp.concatenate(
            [
                rows[pl.ds(window, frequencies, stride=windows), :].astype(jnp.bfloat16)
                for window in (2 * shot, 2 * shot + 1)
            ],
            axis=0,
        )
        turned = lax.dot_general(order, spectra, NT_DIMS, preferred_element_type=jnp.float32).astype(
            jnp.bfloat16
        )
        spans = [slice(half * frequencies, (half + 1) * frequencies) for half in range(2)]
        turned = jnp.concatenate(
            [jnp.concatenate([turned[:receivers, span], turned[receivers:, span]], axis=1) for span in spans],
            axis=0,
        )
        in_time = jnp.dot(turned, inverse[...], preferred_element_type=jnp.float32)
        for half in range(2):
            span = slice(half * taps, (half + 1) * taps)
            result[shot, :, span] = (
                data[shot, :, span] - gain[pl.ds(shot, 1), :] * in_time[half * receivers : (half + 1) * receivers]
            )
        copies.append(pltpu.make_async_copy(result.at[shot], out.at[shot], written.at[shot]))
        copies[-1].start()
    for copy in copies:
        copy.wait()


def on_device(shot_devices, surf_devices, data, positions, plan, primaries, scale):
    shots, receivers, samples = data.shape
    position_count, width, _, taps = primaries.shape
    devices = shot_devices * surf_devices
    forward, inverse = fourier_tables(taps)
    forward, inverse = jnp.asarray(forward), jnp.asarray(inverse)
    chunk = (2 * width * position_count + 2 * 2 * shots * position_count) // LANES
    vmem = pl.BlockSpec(memory_space=pltpu.VMEM)
    hbm = pl.BlockSpec(memory_space=pltpu.HBM)
    limit = pltpu.CompilerParams(vmem_limit_bytes=32 * 1024 * 1024)

    sent, place, gain = pl.pallas_call(
        spectra_kernel,
        out_shape=(
            jax.ShapeDtypeStruct((taps * chunk, LANES), jnp.bfloat16),
            jax.ShapeDtypeStruct((1, LANES), jnp.int32),
            jax.ShapeDtypeStruct((shots, taps), jnp.float32),
        ),
        in_specs=[hbm] * 6,
        out_specs=(vmem, vmem, vmem),
        scratch_shapes=[
            pltpu.VMEM((1, receivers), jnp.int32),
            pltpu.VMEM((1, plan.shape[0]), jnp.int32),
            pltpu.SMEM((shots,), jnp.float32),
            pltpu.VMEM(data.shape, jnp.float32),
            pltpu.VMEM((position_count, width, taps), jnp.bfloat16),
            pltpu.VMEM(forward.shape, jnp.bfloat16),
            pltpu.VMEM((taps // LANES, position_count * width, LANES), jnp.float32),
            pltpu.VMEM((taps * chunk, LANES), jnp.float32),
            pltpu.SemaphoreType.DMA((9,)),
        ],
        compiler_params=limit,
    )(
        *(
            pltpu.with_memory_space_constraint(operand, pltpu.HBM)
            for operand in (
                positions.reshape(1, receivers),
                plan.reshape(1, plan.shape[0]),
                scale,
                data,
                primaries.reshape(position_count, width, taps),
                forward,
            )
        )
    )
    sent = sent.reshape(devices, chunk // 2, 2, LANES)
    received = lax.all_to_all(sent, ("shot", "surf"), 0, 0, tiled=True)
    received = received.reshape(devices * chunk, LANES)

    back = devices * 4

    def product(*refs):
        product_kernel(shot_devices, surf_devices, width, *refs)

    terms = pl.pallas_call(
        product,
        out_shape=jax.ShapeDtypeStruct((back, LANES), jnp.bfloat16),
        in_specs=[vmem],
        out_specs=vmem,
        scratch_shapes=[
            pltpu.VMEM((devices * chunk, LANES), jnp.float32),
            pltpu.VMEM((back, LANES), jnp.float32),
        ],
        compiler_params=limit,
    )(received)
    terms = lax.all_to_all(terms.reshape(devices, 4, LANES), ("shot", "surf"), 0, 0, tiled=True)
    terms = terms.reshape(back, LANES)

    return pl.pallas_call(
        subtract_kernel,
        out_shape=jax.ShapeDtypeStruct(data.shape, jnp.float32),
        in_specs=[vmem] * 5,
        out_specs=hbm,
        scratch_shapes=[
            pltpu.VMEM((back, LANES), jnp.float32),
            pltpu.VMEM(data.shape, jnp.float32),
            pltpu.SemaphoreType.DMA((shots,)),
        ],
        compiler_params=limit,
    )(place, gain, terms, inverse, data)


def solution(mesh):
    P = jax.sharding.PartitionSpec
    shot_devices, surf_devices = mesh.shape["shot"], mesh.shape["surf"]

    def device(*args):
        return on_device(shot_devices, surf_devices, *args)

    in_specs = (P("shot", "surf", None), P("surf"), P(), P("surf", None, "shot", None), P("shot"))
    out_specs = P("shot", "surf", None)
    return jax.shard_map(device, mesh=mesh, in_specs=in_specs, out_specs=out_specs, check_vma=False)
```

```python
import math

import jax
import jax.numpy as jnp
import ml_dtypes
import numpy as np
from jax import lax
from jax.experimental import pallas as pl
from jax.experimental.pallas import tpu as pltpu

LANES = 128
SHOT = ("z2", "z1", "z0", "yh", "core")
SURF = ("x1", "x0", "yl")
ORDER = ("core", "z2", "yh", "z1", "z0", "x1", "x0", "yl")
RUN, RUN_AXES = ("core", "z2", "yh", "z1", "z0"), ()
NT_DIMS = (((1,), (1,)), ((), ()))


def weight(axis):
    return 1 << (len(ORDER) - 1 - ORDER.index(axis))


def offset(axes, index):
    return sum(weight(axis) * (index >> (len(axes) - 1 - i) & 1) for i, axis in enumerate(axes))


def coordinate(axes):
    index = 0
    for axis in axes:
        index = 2 * index + lax.axis_index(axis)
    return index


def fourier_tables(taps):
    length = 2 * taps
    frequency = np.arange(taps)[:, None]
    time = np.arange(length)[None, :]
    angle = (frequency * time % length) * (2.0 * math.pi / length)
    cosine, sine = np.cos(angle), np.sin(angle)
    alternate = 1.0 - 2.0 * (time % 2)
    packed = frequency == 0
    forward = np.concatenate([cosine, np.where(packed, alternate, -sine)], axis=0)[:, :taps]
    weight = np.where(packed, 1.0, 2.0) / length
    inverse_real = (weight * cosine)[:, taps:]
    inverse_imag = np.where(packed, alternate / length, -2.0 * sine / length)[:, taps:]
    inverse = np.concatenate([inverse_real, inverse_imag], axis=0)
    return forward.astype(ml_dtypes.bfloat16), inverse.astype(ml_dtypes.bfloat16)


def exchange_groups(parts):
    lane = lax.broadcasted_iota(jnp.int32, parts[0].shape, 1)
    parts = list(parts)
    for bit in (1, 2):
        shift = bit * 32
        high = (lane & shift) != 0
        swapped = [None] * 4
        for low_index in range(4):
            if low_index & bit:
                continue
            low, top = parts[low_index], parts[low_index | bit]
            swapped[low_index] = jnp.where(high, pltpu.roll(top, shift, 1), low)
            swapped[low_index | bit] = jnp.where(high, top, pltpu.roll(low, LANES - shift, 1))
        parts = swapped
    return parts


def spectra_kernel(
    positions_in,
    plan_in,
    scale_in,
    data_in,
    primaries_in,
    forward_in,
    sent,
    place,
    gain,
    positions,
    plan,
    scale,
    data,
    primaries,
    forward,
    rows,
    packed,
    arrived,
):
    shots, _, samples = data.shape
    position_count, width, taps = primaries.shape
    row_count = position_count * width
    frequencies = taps
    chunk = packed.shape[0] // frequencies
    groups = width // 4

    def halves(far, near):
        half = far.shape[0] // 2
        return [(far.at[pl.ds(i * half, half)], near.at[pl.ds(i * half, half)]) for i in range(2)]

    pairs = halves(primaries_in, primaries) + halves(forward_in, forward) + halves(data_in, data)
    pairs += [(positions_in, positions), (plan_in, plan), (scale_in, scale)]
    copies = [pltpu.make_async_copy(far, near, arrived.at[i]) for i, (far, near) in enumerate(pairs)]
    for copy in copies:
        copy.start()

    for copy in copies[:2]:
        copy.wait()
    flat = primaries[...].reshape(row_count, taps)
    tiles = range(taps // LANES)
    for tile in tiles:
        rows[tile] = flat[:, tile * LANES : (tile + 1) * LANES].astype(jnp.float32)
    for copy in copies[2:4]:
        copy.wait()
    for group in range(groups):
        block = jnp.concatenate(
            [
                jnp.concatenate(
                    [rows[tile, pl.ds(4 * group + j, position_count, stride=width), :] for tile in tiles],
                    axis=1,
                )
                for j in range(4)
            ],
            axis=0,
        ).astype(jnp.bfloat16)
        spectra = lax.dot_general(forward[...], block, NT_DIMS, preferred_element_type=jnp.float32)
        for part in range(2):
            packed[pl.ds(part * groups + group, frequencies, stride=chunk), :] = spectra[
                part * frequencies : (part + 1) * frequencies
            ]

    for copy in copies[4:]:
        copy.wait()
    slots = plan.shape[1]
    lane = lax.broadcasted_iota(jnp.int32, (slots, LANES), 1)
    source = jnp.zeros((slots, LANES), jnp.int32)
    for i, axis in enumerate(RUN_AXES + RUN):
        bit = (lane >> (len(SHOT) - 1 - i)) & 1
        source = source + (bit << (len(SHOT) - 1 - SHOT.index(axis)))
    chosen = (lax.broadcasted_iota(jnp.int32, (slots, LANES), 0) == source).astype(jnp.bfloat16)
    panels = jnp.broadcast_to(plan[...].astype(jnp.bfloat16), (16, slots))
    panel = jnp.dot(panels, chosen, preferred_element_type=jnp.float32)[:1].astype(jnp.int32)
    place[...] = panel + lane[:1] // slots * slots
    for shot in range(shots):
        gain[pl.ds(shot, 1), :] = jnp.full((1, taps), scale[shot], jnp.float32)
    first = coordinate(SURF) * position_count
    position = lax.broadcasted_iota(jnp.int32, (position_count, positions.shape[1]), 0) + first
    onehot = (position == positions[...]).astype(jnp.float32)
    halves_in_time = []
    for shot in range(shots):
        gathered = jnp.dot(
            onehot, data[shot], precision=lax.Precision.HIGHEST, preferred_element_type=jnp.float32
        ).astype(jnp.bfloat16)
        halves_in_time += [gathered[:, :taps], gathered[:, taps:]]
    spectra = lax.dot_general(
        forward[...], jnp.concatenate(halves_in_time, axis=0), NT_DIMS, preferred_element_type=jnp.float32
    )
    odd = lax.broadcasted_iota(jnp.int32, spectra.shape, 0) % 2 == 1
    second = lax.broadcasted_iota(jnp.int32, spectra.shape, 1) % (2 * position_count) >= position_count
    earlier = jnp.where(second, pltpu.roll(spectra, position_count, 1), 0.0)
    spectra = earlier + jnp.where(odd, -spectra, spectra)
    for part in range(2):
        packed[pl.ds(2 * groups + part, frequencies, stride=chunk), :] = spectra[
            part * frequencies : (part + 1) * frequencies
        ]
    sent[...] = packed[...].astype(jnp.bfloat16)


def product_kernel(shot_devices, surf_devices, width, received, sent, rows, packed):
    rows[...] = received[...].astype(jnp.float32)
    chunk = received.shape[0] // (shot_devices * surf_devices)
    groups = width // 4
    run, step = 1 << len(RUN), weight(RUN[-1])
    starts = [offset(RUN_AXES, i) for i in range(1 << len(RUN_AXES))]

    def regrouped(row):
        halves = []
        for half in range(surf_devices // 4):
            parts = [
                jnp.concatenate(
                    [
                        rows[pl.ds((start + offset(SURF, half * 4 + i)) * chunk + row, run, stride=step * chunk), :]
                        for start in starts
                    ],
                    axis=0,
                ).astype(jnp.bfloat16)
                for i in range(4)
            ]
            halves.append(exchange_groups(parts))
        return [jnp.concatenate([half[j] for half in halves], axis=1) for j in range(4)]

    primary = []
    for part in range(2):
        by_receiver = []
        for group in range(groups):
            by_receiver += regrouped(part * groups + group)
        primary.append(by_receiver)
    traces = [jnp.concatenate(regrouped(2 * groups + part), axis=0) for part in range(2)]
    interior = coordinate(ORDER) > 0
    pair = width // surf_devices
    for block in range(surf_devices):
        which = range(pair * block, pair * (block + 1))
        real = jnp.concatenate([primary[0][q] for q in which], axis=0)
        imag = jnp.concatenate([primary[1][q] for q in which], axis=0)
        none = jnp.zeros_like(imag)
        with_real = jnp.concatenate([real, jnp.where(interior, imag, none)], axis=0)
        with_imag = jnp.concatenate(
            [jnp.where(interior, -imag, none), jnp.where(interior, real, imag)], axis=0
        )
        product = lax.dot_general(
            traces[0], with_real, NT_DIMS, preferred_element_type=jnp.float32
        ) + lax.dot_general(traces[1], with_imag, NT_DIMS, preferred_element_type=jnp.float32)
        for window in range(4):
            for i, start in enumerate(starts):
                row = window * shot_devices + i * run
                packed[pl.ds((start + offset(SURF, block)) * 4 + window, run, stride=step * 4), :] = product[
                    row : row + run
                ]
    sent[...] = packed[...].astype(jnp.bfloat16)


def subtract_kernel(place, gain, received, inverse, data, out, rows, result, written):
    shots, receivers, _ = data.shape
    frequencies, taps = inverse.shape[0] // 2, inverse.shape[1]
    windows = received.shape[0] // frequencies
    rows[...] = received[...].astype(jnp.float32)
    order = (lax.broadcasted_iota(jnp.int32, (LANES, LANES), 0) == place[...]).astype(jnp.bfloat16)
    copies = []
    for shot in range(shots):
        spectra = jnp.concatenate(
            [
                rows[pl.ds(window, frequencies, stride=windows), :].astype(jnp.bfloat16)
                for window in (2 * shot, 2 * shot + 1)
            ],
            axis=0,
        )
        turned = lax.dot_general(order, spectra, NT_DIMS, preferred_element_type=jnp.float32).astype(
            jnp.bfloat16
        )
        spans = [slice(half * frequencies, (half + 1) * frequencies) for half in range(2)]
        turned = jnp.concatenate(
            [jnp.concatenate([turned[:receivers, span], turned[receivers:, span]], axis=1) for span in spans],
            axis=0,
        )
        in_time = jnp.dot(turned, inverse[...], preferred_element_type=jnp.float32)
        for half in range(2):
            span = slice(half * taps, (half + 1) * taps)
            result[shot, :, span] = (
                data[shot, :, span] - gain[pl.ds(shot, 1), :] * in_time[half * receivers : (half + 1) * receivers]
            )
        copies.append(pltpu.make_async_copy(result.at[shot], out.at[shot], written.at[shot]))
        copies[-1].start()
    for copy in copies:
        copy.wait()


def on_device(shot_devices, surf_devices, data, positions, plan, primaries, scale):
    shots, receivers, samples = data.shape
    position_count, width, _, taps = primaries.shape
    devices = shot_devices * surf_devices
    forward, inverse = fourier_tables(taps)
    forward, inverse = jnp.asarray(forward), jnp.asarray(inverse)
    chunk = (2 * width * position_count + 2 * 2 * shots * position_count) // LANES
    vmem = pl.BlockSpec(memory_space=pltpu.VMEM)
    hbm = pl.BlockSpec(memory_space=pltpu.HBM)
    limit = pltpu.CompilerParams(vmem_limit_bytes=32 * 1024 * 1024)

    sent, place, gain = pl.pallas_call(
        spectra_kernel,
        out_shape=(
            jax.ShapeDtypeStruct((taps * chunk, LANES), jnp.bfloat16),
            jax.ShapeDtypeStruct((1, LANES), jnp.int32),
            jax.ShapeDtypeStruct((shots, taps), jnp.float32),
        ),
        in_specs=[hbm] * 6,
        out_specs=(vmem, vmem, vmem),
        scratch_shapes=[
            pltpu.VMEM((1, receivers), jnp.int32),
            pltpu.VMEM((1, plan.shape[0]), jnp.int32),
            pltpu.SMEM((shots,), jnp.float32),
            pltpu.VMEM(data.shape, jnp.float32),
            pltpu.VMEM((position_count, width, taps), jnp.bfloat16),
            pltpu.VMEM(forward.shape, jnp.bfloat16),
            pltpu.VMEM((taps // LANES, position_count * width, LANES), jnp.float32),
            pltpu.VMEM((taps * chunk, LANES), jnp.float32),
            pltpu.SemaphoreType.DMA((9,)),
        ],
        compiler_params=limit,
    )(
        *(
            pltpu.with_memory_space_constraint(operand, pltpu.HBM)
            for operand in (
                positions.reshape(1, receivers),
                plan.reshape(1, plan.shape[0]),
                scale,
                data,
                primaries.reshape(position_count, width, taps),
                forward,
            )
        )
    )
    sent = sent.reshape(devices, chunk // 2, 2, LANES)
    received = lax.all_to_all(sent, ORDER, 0, 0, tiled=True)
    received = received.reshape(devices * chunk, LANES)

    back = devices * 4

    def product(*refs):
        product_kernel(shot_devices, surf_devices, width, *refs)

    terms = pl.pallas_call(
        product,
        out_shape=jax.ShapeDtypeStruct((back, LANES), jnp.bfloat16),
        in_specs=[vmem],
        out_specs=vmem,
        scratch_shapes=[
            pltpu.VMEM((devices * chunk, LANES), jnp.float32),
            pltpu.VMEM((back, LANES), jnp.float32),
        ],
        compiler_params=limit,
    )(received)
    terms = lax.all_to_all(terms.reshape(devices, 4, LANES), ORDER, 0, 0, tiled=True)
    terms = terms.reshape(back, LANES)

    return pl.pallas_call(
        subtract_kernel,
        out_shape=jax.ShapeDtypeStruct(data.shape, jnp.float32),
        in_specs=[vmem] * 5,
        out_specs=hbm,
        scratch_shapes=[
            pltpu.VMEM((back, LANES), jnp.float32),
            pltpu.VMEM(data.shape, jnp.float32),
            pltpu.SemaphoreType.DMA((shots,)),
        ],
        compiler_params=limit,
    )(place, gain, terms, inverse, data)


def solution(mesh):
    P = jax.sharding.PartitionSpec
    shot_devices, surf_devices = mesh.shape["shot"], mesh.shape["surf"]
    axes = SHOT + SURF
    fine = jax.sharding.Mesh(mesh.devices.reshape((2,) * len(axes)), axes)

    def device(*args):
        return on_device(shot_devices, surf_devices, *args)

    in_specs = (P(SHOT, SURF, None), P(SURF), P(), P(SURF, None, SHOT, None), P(SHOT))
    out_specs = P(SHOT, SURF, None)
    return jax.shard_map(device, mesh=fine, in_specs=in_specs, out_specs=out_specs, check_vma=False)
```

```python
import math

import jax
import jax.numpy as jnp
import ml_dtypes
import numpy as np
from jax import lax
from jax.experimental import pallas as pl
from jax.experimental.pallas import tpu as pltpu

LANES = 128
SHOT = ("z2", "z1", "z0", "yh", "core")
SURF = ("x1", "x0", "yl")
ORDER = ("core", "z2", "yh", "z1", "z0", "x1", "x0", "yl")
RUN, RUN_AXES = ("core", "z2", "yh", "z1", "z0"), ()
NT_DIMS = (((1,), (1,)), ((), ()))


def weight(axis):
    return 1 << (len(ORDER) - 1 - ORDER.index(axis))


def offset(axes, index):
    return sum(weight(axis) * (index >> (len(axes) - 1 - i) & 1) for i, axis in enumerate(axes))


def coordinate(axes):
    index = 0
    for axis in axes:
        index = 2 * index + lax.axis_index(axis)
    return index


def fourier_tables(taps):
    length = 2 * taps
    frequency = np.arange(taps)[:, None]
    time = np.arange(length)[None, :]
    angle = (frequency * time % length) * (2.0 * math.pi / length)
    cosine, sine = np.cos(angle), np.sin(angle)
    alternate = 1.0 - 2.0 * (time % 2)
    packed = frequency == 0
    forward = np.concatenate([cosine, np.where(packed, alternate, -sine)], axis=0)[:, :taps]
    weight = np.where(packed, 1.0, 2.0) / length
    inverse_real = (weight * cosine)[:, taps:]
    inverse_imag = np.where(packed, alternate / length, -2.0 * sine / length)[:, taps:]
    inverse = np.concatenate([inverse_real, inverse_imag], axis=0)
    return forward.astype(ml_dtypes.bfloat16), inverse.astype(ml_dtypes.bfloat16)


def exchange_groups(parts):
    lane = lax.broadcasted_iota(jnp.int32, parts[0].shape, 1)
    parts = list(parts)
    for bit in (1, 2):
        shift = bit * 32
        high = (lane & shift) != 0
        swapped = [None] * 4
        for low_index in range(4):
            if low_index & bit:
                continue
            low, top = parts[low_index], parts[low_index | bit]
            swapped[low_index] = jnp.where(high, pltpu.roll(top, shift, 1), low)
            swapped[low_index | bit] = jnp.where(high, top, pltpu.roll(low, LANES - shift, 1))
        parts = swapped
    return parts


def spectra_kernel(
    positions_in,
    plan_in,
    scale_in,
    data_in,
    primaries_in,
    forward_in,
    sent,
    place,
    gain,
    positions,
    plan,
    scale,
    data,
    primaries,
    forward,
    rows,
    packed,
    arrived,
):
    shots, _, samples = data.shape
    position_count, width, taps = primaries.shape
    row_count = position_count * width
    frequencies = taps
    chunk = packed.shape[0] // frequencies
    groups = width // 4

    pairs = [(data_in, data), (positions_in, positions), (primaries_in, primaries), (forward_in, forward)]
    pairs += [(plan_in, plan), (scale_in, scale)]
    copies = [pltpu.make_async_copy(far, near, arrived.at[i]) for i, (far, near) in enumerate(pairs)]
    for copy in copies:
        copy.start()

    for copy in copies[:1]:
        copy.wait()
    copies[1].wait()
    first = coordinate(SURF) * position_count
    receivers = positions.shape[1]
    position = lax.broadcasted_iota(jnp.int32, (position_count, receivers), 0) + first
    onehot = (position == positions[...]).astype(jnp.bfloat16)
    onehot = jnp.concatenate([onehot] * 3, axis=1)
    halves_in_time = []
    for shot in range(shots):
        parts, rest = [], data[shot]
        for _ in range(3):
            parts.append(rest.astype(jnp.bfloat16))
            rest = rest - parts[-1].astype(jnp.float32)
        gathered = jnp.dot(
            onehot, jnp.concatenate(parts, axis=0), preferred_element_type=jnp.float32
        ).astype(jnp.bfloat16)
        halves_in_time += [gathered[:, :taps], gathered[:, taps:]]

    for copy in copies[2:3]:
        copy.wait()
    flat = primaries[...].reshape(row_count, taps)
    tiles = range(taps // LANES)
    for tile in tiles:
        rows[tile] = flat[:, tile * LANES : (tile + 1) * LANES].astype(jnp.float32)
    for copy in copies[3:4]:
        copy.wait()
    for group in range(groups):
        block = jnp.concatenate(
            [
                jnp.concatenate(
                    [rows[tile, pl.ds(4 * group + j, position_count, stride=width), :] for tile in tiles],
                    axis=1,
                )
                for j in range(4)
            ],
            axis=0,
        ).astype(jnp.bfloat16)
        spectra = lax.dot_general(forward[...], block, NT_DIMS, preferred_element_type=jnp.float32)
        for part in range(2):
            packed[pl.ds(part * groups + group, frequencies, stride=chunk), :] = spectra[
                part * frequencies : (part + 1) * frequencies
            ]

    for copy in copies[4:]:
        copy.wait()
    slots = plan.shape[1]
    lane = lax.broadcasted_iota(jnp.int32, (slots, LANES), 1)
    source = jnp.zeros((slots, LANES), jnp.int32)
    for i, axis in enumerate(RUN_AXES + RUN):
        bit = (lane >> (len(SHOT) - 1 - i)) & 1
        source = source + (bit << (len(SHOT) - 1 - SHOT.index(axis)))
    chosen = (lax.broadcasted_iota(jnp.int32, (slots, LANES), 0) == source).astype(jnp.bfloat16)
    panels = jnp.broadcast_to(plan[...].astype(jnp.bfloat16), (16, slots))
    panel = jnp.dot(panels, chosen, preferred_element_type=jnp.float32)[:1].astype(jnp.int32)
    place[...] = panel + lane[:1] // slots * slots
    for shot in range(shots):
        gain[pl.ds(shot, 1), :] = jnp.full((1, taps), scale[shot], jnp.float32)
    spectra = lax.dot_general(
        forward[...], jnp.concatenate(halves_in_time, axis=0), NT_DIMS, preferred_element_type=jnp.float32
    )
    odd = lax.broadcasted_iota(jnp.int32, spectra.shape, 0) % 2 == 1
    second = lax.broadcasted_iota(jnp.int32, spectra.shape, 1) % (2 * position_count) >= position_count
    earlier = jnp.where(second, pltpu.roll(spectra, position_count, 1), 0.0)
    spectra = earlier + jnp.where(odd, -spectra, spectra)
    for part in range(2):
        packed[pl.ds(2 * groups + part, frequencies, stride=chunk), :] = spectra[
            part * frequencies : (part + 1) * frequencies
        ]
    sent[...] = packed[...].astype(jnp.bfloat16)


def product_kernel(shot_devices, surf_devices, width, received, sent, rows, packed):
    rows[...] = received[...].astype(jnp.float32)
    chunk = received.shape[0] // (shot_devices * surf_devices)
    groups = width // 4
    run, step = 1 << len(RUN), weight(RUN[-1])
    starts = [offset(RUN_AXES, i) for i in range(1 << len(RUN_AXES))]

    def regrouped(row):
        halves = []
        for half in range(surf_devices // 4):
            parts = [
                jnp.concatenate(
                    [
                        rows[pl.ds((start + offset(SURF, half * 4 + i)) * chunk + row, run, stride=step * chunk), :]
                        for start in starts
                    ],
                    axis=0,
                ).astype(jnp.bfloat16)
                for i in range(4)
            ]
            halves.append(exchange_groups(parts))
        return [jnp.concatenate([half[j] for half in halves], axis=1) for j in range(4)]

    primary = []
    for part in range(2):
        by_receiver = []
        for group in range(groups):
            by_receiver += regrouped(part * groups + group)
        primary.append(by_receiver)
    traces = [jnp.concatenate(regrouped(2 * groups + part), axis=0) for part in range(2)]
    interior = coordinate(ORDER) > 0
    pair = width // surf_devices
    for block in range(surf_devices):
        which = range(pair * block, pair * (block + 1))
        real = jnp.concatenate([primary[0][q] for q in which], axis=0)
        imag = jnp.concatenate([primary[1][q] for q in which], axis=0)
        none = jnp.zeros_like(imag)
        with_real = jnp.concatenate([real, jnp.where(interior, imag, none)], axis=0)
        with_imag = jnp.concatenate(
            [jnp.where(interior, -imag, none), jnp.where(interior, real, imag)], axis=0
        )
        product = lax.dot_general(
            traces[0], with_real, NT_DIMS, preferred_element_type=jnp.float32
        ) + lax.dot_general(traces[1], with_imag, NT_DIMS, preferred_element_type=jnp.float32)
        for window in range(4):
            for i, start in enumerate(starts):
                row = window * shot_devices + i * run
                packed[pl.ds((start + offset(SURF, block)) * 4 + window, run, stride=step * 4), :] = product[
                    row : row + run
                ]
    sent[...] = packed[...].astype(jnp.bfloat16)


def subtract_kernel(place, gain, received, inverse, data, out, rows, result, written):
    shots, receivers, _ = data.shape
    frequencies, taps = inverse.shape[0] // 2, inverse.shape[1]
    windows = received.shape[0] // frequencies
    rows[...] = received[...].astype(jnp.float32)
    order = (lax.broadcasted_iota(jnp.int32, (LANES, LANES), 0) == place[...]).astype(jnp.bfloat16)
    copies = []
    for shot in range(shots):
        spectra = jnp.concatenate(
            [
                rows[pl.ds(window, frequencies, stride=windows), :].astype(jnp.bfloat16)
                for window in (2 * shot, 2 * shot + 1)
            ],
            axis=0,
        )
        turned = lax.dot_general(order, spectra, NT_DIMS, preferred_element_type=jnp.float32).astype(
            jnp.bfloat16
        )
        spans = [slice(half * frequencies, (half + 1) * frequencies) for half in range(2)]
        turned = jnp.concatenate(
            [jnp.concatenate([turned[:receivers, span], turned[receivers:, span]], axis=1) for span in spans],
            axis=0,
        )
        in_time = jnp.dot(turned, inverse[...], preferred_element_type=jnp.float32)
        for half in range(2):
            span = slice(half * taps, (half + 1) * taps)
            result[shot, :, span] = (
                data[shot, :, span] - gain[pl.ds(shot, 1), :] * in_time[half * receivers : (half + 1) * receivers]
            )
        copies.append(pltpu.make_async_copy(result.at[shot], out.at[shot], written.at[shot]))
        copies[-1].start()
    for copy in copies:
        copy.wait()


def on_device(shot_devices, surf_devices, data, positions, plan, primaries, scale):
    shots, receivers, samples = data.shape
    position_count, width, _, taps = primaries.shape
    devices = shot_devices * surf_devices
    forward, inverse = fourier_tables(taps)
    forward, inverse = jnp.asarray(forward), jnp.asarray(inverse)
    chunk = (2 * width * position_count + 2 * 2 * shots * position_count) // LANES
    vmem = pl.BlockSpec(memory_space=pltpu.VMEM)
    hbm = pl.BlockSpec(memory_space=pltpu.HBM)
    limit = pltpu.CompilerParams(vmem_limit_bytes=32 * 1024 * 1024)

    sent, place, gain = pl.pallas_call(
        spectra_kernel,
        out_shape=(
            jax.ShapeDtypeStruct((taps * chunk, LANES), jnp.bfloat16),
            jax.ShapeDtypeStruct((1, LANES), jnp.int32),
            jax.ShapeDtypeStruct((shots, taps), jnp.float32),
        ),
        in_specs=[hbm] * 6,
        out_specs=(vmem, vmem, vmem),
        scratch_shapes=[
            pltpu.VMEM((1, receivers), jnp.int32),
            pltpu.VMEM((1, plan.shape[0]), jnp.int32),
            pltpu.SMEM((shots,), jnp.float32),
            pltpu.VMEM(data.shape, jnp.float32),
            pltpu.VMEM((position_count, width, taps), jnp.bfloat16),
            pltpu.VMEM(forward.shape, jnp.bfloat16),
            pltpu.VMEM((taps // LANES, position_count * width, LANES), jnp.float32),
            pltpu.VMEM((taps * chunk, LANES), jnp.float32),
            pltpu.SemaphoreType.DMA((6,)),
        ],
        compiler_params=limit,
    )(
        *(
            pltpu.with_memory_space_constraint(operand, pltpu.HBM)
            for operand in (
                positions.reshape(1, receivers),
                plan.reshape(1, plan.shape[0]),
                scale,
                data,
                primaries.reshape(position_count, width, taps),
                forward,
            )
        )
    )
    sent = sent.reshape(devices, chunk // 2, 2, LANES)
    received = lax.all_to_all(sent, ORDER, 0, 0, tiled=True)
    received = received.reshape(devices * chunk, LANES)

    back = devices * 4

    def product(*refs):
        product_kernel(shot_devices, surf_devices, width, *refs)

    terms = pl.pallas_call(
        product,
        out_shape=jax.ShapeDtypeStruct((back, LANES), jnp.bfloat16),
        in_specs=[vmem],
        out_specs=vmem,
        scratch_shapes=[
            pltpu.VMEM((devices * chunk, LANES), jnp.float32),
            pltpu.VMEM((back, LANES), jnp.float32),
        ],
        compiler_params=limit,
    )(received)
    terms = lax.all_to_all(terms.reshape(devices, 4, LANES), ORDER, 0, 0, tiled=True)
    terms = terms.reshape(back, LANES)

    return pl.pallas_call(
        subtract_kernel,
        out_shape=jax.ShapeDtypeStruct(data.shape, jnp.float32),
        in_specs=[vmem] * 5,
        out_specs=hbm,
        scratch_shapes=[
            pltpu.VMEM((back, LANES), jnp.float32),
            pltpu.VMEM(data.shape, jnp.float32),
            pltpu.SemaphoreType.DMA((shots,)),
        ],
        compiler_params=limit,
    )(place, gain, terms, inverse, data)


def solution(mesh):
    P = jax.sharding.PartitionSpec
    shot_devices, surf_devices = mesh.shape["shot"], mesh.shape["surf"]
    axes = SHOT + SURF
    fine = jax.sharding.Mesh(mesh.devices.reshape((2,) * len(axes)), axes)

    def device(*args):
        return on_device(shot_devices, surf_devices, *args)

    in_specs = (P(SHOT, SURF, None), P(SURF), P(), P(SURF, None, SHOT, None), P(SHOT))
    out_specs = P(SHOT, SURF, None)
    return jax.shard_map(device, mesh=fine, in_specs=in_specs, out_specs=out_specs, check_vma=False)
```

```python
import math

import jax
import jax.numpy as jnp
import ml_dtypes
import numpy as np
from jax import lax
from jax.experimental import pallas as pl
from jax.experimental.pallas import tpu as pltpu

LANES = 128
SHOT = ("z2", "z1", "z0", "yh", "core")
SURF = ("x1", "x0", "yl")
ORDER = ("core", "z2", "yh", "z1", "z0", "x1", "x0", "yl")
RUN, RUN_AXES = ("core", "z2", "yh", "z1", "z0"), ()
NT_DIMS = (((1,), (1,)), ((), ()))


def weight(axis):
    return 1 << (len(ORDER) - 1 - ORDER.index(axis))


def offset(axes, index):
    return sum(weight(axis) * (index >> (len(axes) - 1 - i) & 1) for i, axis in enumerate(axes))


def coordinate(axes):
    index = 0
    for axis in axes:
        index = 2 * index + lax.axis_index(axis)
    return index


def fourier_tables(taps):
    length = 2 * taps
    frequency = np.arange(taps)[:, None]
    time = np.arange(length)[None, :]
    angle = (frequency * time % length) * (2.0 * math.pi / length)
    cosine, sine = np.cos(angle), np.sin(angle)
    alternate = 1.0 - 2.0 * (time % 2)
    packed = frequency == 0
    forward = np.concatenate([cosine, np.where(packed, alternate, -sine)], axis=0)[:, :taps]
    weight = np.where(packed, 1.0, 2.0) / length
    inverse_real = (weight * cosine)[:, taps:]
    inverse_imag = np.where(packed, alternate / length, -2.0 * sine / length)[:, taps:]
    inverse = np.concatenate([inverse_real, inverse_imag], axis=0)
    return forward.astype(ml_dtypes.bfloat16), inverse.astype(ml_dtypes.bfloat16)


def exchange_groups(parts):
    lane = lax.broadcasted_iota(jnp.int32, parts[0].shape, 1)
    parts = list(parts)
    for bit in (1, 2):
        shift = bit * 32
        high = (lane & shift) != 0
        swapped = [None] * 4
        for low_index in range(4):
            if low_index & bit:
                continue
            low, top = parts[low_index], parts[low_index | bit]
            swapped[low_index] = jnp.where(high, pltpu.roll(top, shift, 1), low)
            swapped[low_index | bit] = jnp.where(high, top, pltpu.roll(low, LANES - shift, 1))
        parts = swapped
    return parts


def spectra_kernel(
    positions_in,
    plan_in,
    scale_in,
    data_in,
    primaries_in,
    forward_in,
    sent,
    place,
    gain,
    positions,
    plan,
    scale,
    data,
    primaries,
    forward,
    rows,
    packed,
    arrived,
):
    shots, _, samples = data.shape
    position_count, width, taps = primaries.shape
    row_count = position_count * width
    frequencies = taps
    chunk = packed.shape[0] // frequencies
    groups = width // 4

    spans = [pl.ds(part * frequencies, frequencies) for part in range(2)]
    pairs = [(data_in, data), (positions_in, positions), (primaries_in, primaries)]
    pairs += [(forward_in.at[span], forward.at[span]) for span in spans]
    pairs += [(plan_in, plan), (scale_in, scale)]
    copies = [pltpu.make_async_copy(far, near, arrived.at[i]) for i, (far, near) in enumerate(pairs)]
    for copy in copies:
        copy.start()

    for copy in copies[:1]:
        copy.wait()
    copies[1].wait()
    first = coordinate(SURF) * position_count
    receivers = positions.shape[1]
    position = lax.broadcasted_iota(jnp.int32, (position_count, receivers), 0) + first
    onehot = (position == positions[...]).astype(jnp.bfloat16)
    onehot = jnp.concatenate([onehot] * 3, axis=1)
    halves_in_time = []
    for shot in range(shots):
        parts, rest = [], data[shot]
        for _ in range(3):
            parts.append(rest.astype(jnp.bfloat16))
            rest = rest - parts[-1].astype(jnp.float32)
        gathered = jnp.dot(
            onehot, jnp.concatenate(parts, axis=0), preferred_element_type=jnp.float32
        ).astype(jnp.bfloat16)
        halves_in_time += [gathered[:, :taps], gathered[:, taps:]]

    for copy in copies[2:3]:
        copy.wait()
    flat = primaries[...].reshape(row_count, taps)
    tiles = range(taps // LANES)
    for tile in tiles:
        rows[tile] = flat[:, tile * LANES : (tile + 1) * LANES].astype(jnp.float32)
    blocks = []
    for group in range(groups):
        block = jnp.concatenate(
            [
                jnp.concatenate(
                    [rows[tile, pl.ds(4 * group + j, position_count, stride=width), :] for tile in tiles],
                    axis=1,
                )
                for j in range(4)
            ],
            axis=0,
        ).astype(jnp.bfloat16)
        blocks.append(block)
    for part, span in enumerate(spans):
        copies[3 + part].wait()
        for group, block in enumerate(blocks):
            packed[pl.ds(part * groups + group, frequencies, stride=chunk), :] = lax.dot_general(
                forward[span, :], block, NT_DIMS, preferred_element_type=jnp.float32
            )

    for copy in copies[5:]:
        copy.wait()
    slots = plan.shape[1]
    lane = lax.broadcasted_iota(jnp.int32, (slots, LANES), 1)
    source = jnp.zeros((slots, LANES), jnp.int32)
    for i, axis in enumerate(RUN_AXES + RUN):
        bit = (lane >> (len(SHOT) - 1 - i)) & 1
        source = source + (bit << (len(SHOT) - 1 - SHOT.index(axis)))
    chosen = (lax.broadcasted_iota(jnp.int32, (slots, LANES), 0) == source).astype(jnp.bfloat16)
    panels = jnp.broadcast_to(plan[...].astype(jnp.bfloat16), (16, slots))
    panel = jnp.dot(panels, chosen, preferred_element_type=jnp.float32)[:1].astype(jnp.int32)
    place[...] = panel + lane[:1] // slots * slots
    for shot in range(shots):
        gain[pl.ds(shot, 1), :] = jnp.full((1, taps), scale[shot], jnp.float32)
    spectra = lax.dot_general(
        forward[...], jnp.concatenate(halves_in_time, axis=0), NT_DIMS, preferred_element_type=jnp.float32
    )
    odd = lax.broadcasted_iota(jnp.int32, spectra.shape, 0) % 2 == 1
    second = lax.broadcasted_iota(jnp.int32, spectra.shape, 1) % (2 * position_count) >= position_count
    earlier = jnp.where(second, pltpu.roll(spectra, position_count, 1), 0.0)
    spectra = earlier + jnp.where(odd, -spectra, spectra)
    for part in range(2):
        packed[pl.ds(2 * groups + part, frequencies, stride=chunk), :] = spectra[
            part * frequencies : (part + 1) * frequencies
        ]
    sent[...] = packed[...].astype(jnp.bfloat16)


def product_kernel(shot_devices, surf_devices, width, received, sent, rows, packed):
    rows[...] = received[...].astype(jnp.float32)
    chunk = received.shape[0] // (shot_devices * surf_devices)
    groups = width // 4
    run, step = 1 << len(RUN), weight(RUN[-1])
    starts = [offset(RUN_AXES, i) for i in range(1 << len(RUN_AXES))]

    def regrouped(row):
        halves = []
        for half in range(surf_devices // 4):
            parts = [
                jnp.concatenate(
                    [
                        rows[pl.ds((start + offset(SURF, half * 4 + i)) * chunk + row, run, stride=step * chunk), :]
                        for start in starts
                    ],
                    axis=0,
                ).astype(jnp.bfloat16)
                for i in range(4)
            ]
            halves.append(exchange_groups(parts))
        return [jnp.concatenate([half[j] for half in halves], axis=1) for j in range(4)]

    primary = []
    for part in range(2):
        by_receiver = []
        for group in range(groups):
            by_receiver += regrouped(part * groups + group)
        primary.append(by_receiver)
    traces = [jnp.concatenate(regrouped(2 * groups + part), axis=0) for part in range(2)]
    interior = coordinate(ORDER) > 0
    pair = width // surf_devices
    for block in range(surf_devices):
        which = range(pair * block, pair * (block + 1))
        real = jnp.concatenate([primary[0][q] for q in which], axis=0)
        imag = jnp.concatenate([primary[1][q] for q in which], axis=0)
        none = jnp.zeros_like(imag)
        with_real = jnp.concatenate([real, jnp.where(interior, imag, none)], axis=0)
        with_imag = jnp.concatenate(
            [jnp.where(interior, -imag, none), jnp.where(interior, real, imag)], axis=0
        )
        product = lax.dot_general(
            traces[0], with_real, NT_DIMS, preferred_element_type=jnp.float32
        ) + lax.dot_general(traces[1], with_imag, NT_DIMS, preferred_element_type=jnp.float32)
        for window in range(4):
            for i, start in enumerate(starts):
                row = window * shot_devices + i * run
                packed[pl.ds((start + offset(SURF, block)) * 4 + window, run, stride=step * 4), :] = product[
                    row : row + run
                ]
    sent[...] = packed[...].astype(jnp.bfloat16)


def subtract_kernel(place, gain, received, inverse, data, out, rows, result, written):
    shots, receivers, _ = data.shape
    frequencies, taps = inverse.shape[0] // 2, inverse.shape[1]
    windows = received.shape[0] // frequencies
    rows[...] = received[...].astype(jnp.float32)
    order = (lax.broadcasted_iota(jnp.int32, (LANES, LANES), 0) == place[...]).astype(jnp.bfloat16)
    copies = []
    for shot in range(shots):
        spectra = jnp.concatenate(
            [
                rows[pl.ds(window, frequencies, stride=windows), :].astype(jnp.bfloat16)
                for window in (2 * shot, 2 * shot + 1)
            ],
            axis=0,
        )
        turned = lax.dot_general(order, spectra, NT_DIMS, preferred_element_type=jnp.float32).astype(
            jnp.bfloat16
        )
        spans = [slice(half * frequencies, (half + 1) * frequencies) for half in range(2)]
        turned = jnp.concatenate(
            [jnp.concatenate([turned[:receivers, span], turned[receivers:, span]], axis=1) for span in spans],
            axis=0,
        )
        in_time = jnp.dot(turned, inverse[...], preferred_element_type=jnp.float32)
        for half in range(2):
            span = slice(half * taps, (half + 1) * taps)
            result[shot, :, span] = (
                data[shot, :, span] - gain[pl.ds(shot, 1), :] * in_time[half * receivers : (half + 1) * receivers]
            )
        copies.append(pltpu.make_async_copy(result.at[shot], out.at[shot], written.at[shot]))
        copies[-1].start()
    for copy in copies:
        copy.wait()


def on_device(shot_devices, surf_devices, data, positions, plan, primaries, scale):
    shots, receivers, samples = data.shape
    position_count, width, _, taps = primaries.shape
    devices = shot_devices * surf_devices
    forward, inverse = fourier_tables(taps)
    forward, inverse = jnp.asarray(forward), jnp.asarray(inverse)
    chunk = (2 * width * position_count + 2 * 2 * shots * position_count) // LANES
    vmem = pl.BlockSpec(memory_space=pltpu.VMEM)
    hbm = pl.BlockSpec(memory_space=pltpu.HBM)
    limit = pltpu.CompilerParams(vmem_limit_bytes=32 * 1024 * 1024)

    sent, place, gain = pl.pallas_call(
        spectra_kernel,
        out_shape=(
            jax.ShapeDtypeStruct((taps * chunk, LANES), jnp.bfloat16),
            jax.ShapeDtypeStruct((1, LANES), jnp.int32),
            jax.ShapeDtypeStruct((shots, taps), jnp.float32),
        ),
        in_specs=[hbm] * 6,
        out_specs=(vmem, vmem, vmem),
        scratch_shapes=[
            pltpu.VMEM((1, receivers), jnp.int32),
            pltpu.VMEM((1, plan.shape[0]), jnp.int32),
            pltpu.SMEM((shots,), jnp.float32),
            pltpu.VMEM(data.shape, jnp.float32),
            pltpu.VMEM((position_count, width, taps), jnp.bfloat16),
            pltpu.VMEM(forward.shape, jnp.bfloat16),
            pltpu.VMEM((taps // LANES, position_count * width, LANES), jnp.float32),
            pltpu.VMEM((taps * chunk, LANES), jnp.float32),
            pltpu.SemaphoreType.DMA((7,)),
        ],
        compiler_params=limit,
    )(
        *(
            pltpu.with_memory_space_constraint(operand, pltpu.HBM)
            for operand in (
                positions.reshape(1, receivers),
                plan.reshape(1, plan.shape[0]),
                scale,
                data,
                primaries.reshape(position_count, width, taps),
                forward,
            )
        )
    )
    sent = sent.reshape(devices, chunk // 2, 2, LANES)
    received = lax.all_to_all(sent, ORDER, 0, 0, tiled=True)
    received = received.reshape(devices * chunk, LANES)

    back = devices * 4

    def product(*refs):
        product_kernel(shot_devices, surf_devices, width, *refs)

    terms = pl.pallas_call(
        product,
        out_shape=jax.ShapeDtypeStruct((back, LANES), jnp.bfloat16),
        in_specs=[vmem],
        out_specs=vmem,
        scratch_shapes=[
            pltpu.VMEM((devices * chunk, LANES), jnp.float32),
            pltpu.VMEM((back, LANES), jnp.float32),
        ],
        compiler_params=limit,
    )(received)
    terms = lax.all_to_all(terms.reshape(devices, 4, LANES), ORDER, 0, 0, tiled=True)
    terms = terms.reshape(back, LANES)

    return pl.pallas_call(
        subtract_kernel,
        out_shape=jax.ShapeDtypeStruct(data.shape, jnp.float32),
        in_specs=[vmem] * 5,
        out_specs=hbm,
        scratch_shapes=[
            pltpu.VMEM((back, LANES), jnp.float32),
            pltpu.VMEM(data.shape, jnp.float32),
            pltpu.SemaphoreType.DMA((shots,)),
        ],
        compiler_params=limit,
    )(place, gain, terms, inverse, data)


def solution(mesh):
    P = jax.sharding.PartitionSpec
    shot_devices, surf_devices = mesh.shape["shot"], mesh.shape["surf"]
    axes = SHOT + SURF
    fine = jax.sharding.Mesh(mesh.devices.reshape((2,) * len(axes)), axes)

    def device(*args):
        return on_device(shot_devices, surf_devices, *args)

    in_specs = (P(SHOT, SURF, None), P(SURF), P(), P(SURF, None, SHOT, None), P(SHOT))
    out_specs = P(SHOT, SURF, None)
    return jax.shard_map(device, mesh=fine, in_specs=in_specs, out_specs=out_specs, check_vma=False)
```
